32 devices in a mesh: dp: 4 (over y, x), expert: 8 (over z, core).
Axes of the slice: x: 2, y: 2, z: 4, core: 2. Of those that a mesh axis runs over, the one named last changes fastest.
Arguments:
- tokens: bfloat16 [1024, 4096], P('expert'), may hold values from -6 to 6
- w_gate: bfloat16 [64, 4096, 1536], P('expert', None, 'dp'), may hold values from -0.09375 to 0.09375
- w_up: bfloat16 [64, 4096, 1536], P('expert', None, 'dp'), may hold values from -0.09375 to 0.09375
- w_down: bfloat16 [64, 1536, 4096], P('expert', 'dp'), may hold values from -0.15625 to 0.15625
- route_ids: int32 [1024, 8], P('expert'), may hold values from 0 to 63, all different within a row; in each aligned block of 128 rows (0 to 127, 128 to 255, ...) at most 24 rows name the same one
- route_weight: float32 [1024, 8], P('expert'), may hold values from 0.1 to 1
Outputs:
- mixed: bfloat16 [1024, 4096], P('expert', 'dp')
The draws below stay inside these ranges and needn't reach their ends.
Inputs may be any that keep to these rules, and one draw needn't show every extreme that they name: `route_ids`: each row names 8 different experts. Within each aligned block of 128 rows (the rows of one device) no expert is named more than 24 times, and in every draw some expert is named exactly 24 times in some block.
All inputs are finite; a program needn't handle non-finite values.
Results may differ from the reference program's by a relative error of at most 0.013.
Values may be sent and summed in bfloat16 or wider, within the bound.
A program may use at most 256 MiB of HBM per device.

```python
import math
import jax
import jax.numpy as jnp
import numpy as np
from jax import lax

D = 4096
HID = 1536
EXPERTS = 64
TOPK = 8
TOK_DEV = 128
TOKENS = 1024
HPART = 384
CAP = 24
N_DP = 4


def level_of(key, extent, split, low, top_value):
    def one(axis_at, blocks):
        draws = jax.random.uniform(jax.random.fold_in(jax.random.fold_in(key, 6), axis_at), (blocks,), jnp.float32, low / len(split), top_value / len(split))
        return jnp.repeat(jnp.exp(draws), extent[axis_at] // blocks).reshape((-1,) + (1,) * (len(extent) - axis_at - 1))

    gain = one(*split[0])
    for cut in split[1:]:
        gain = gain * one(*cut)
    return gain


def shared_out(stream_key, own, number, rows, count, top, most, lean):
    sequence = jax.random.permutation(stream_key, count)
    crowded, common = shares(count, rows * top, most, lean, True), shares(count, rows * top, most, lean, False)
    places = jnp.arange(count)

    def named(lengths, rotation):
        used = int((lengths > 0).sum())
        fixed = max(1, used // 4)
        shifted = fixed + (places - fixed + rotation * (used - fixed)) % max(1, count - fixed)
        return jnp.zeros((count,), jnp.int32).at[sequence[jnp.where(places < fixed, places, shifted)]].set(jnp.asarray(lengths, jnp.int32))

    lengths = jnp.where(number % 4 == 0, named(crowded, number // 4), named(common, number - number // 4 - 1))
    mixed = jax.random.permutation(jax.random.fold_in(own, 3), count)
    giver, sink = mixed[0:count // 2 * 2:2], mixed[1:count // 2 * 2:2]
    room = jnp.minimum(lengths[giver] - 1, most - lengths[sink]) // 2
    room = jnp.where((giver == sequence[0]) | (sink == sequence[0]) | (lengths[sink] == 0), 0, jnp.maximum(room, 0))
    shifted = jax.random.randint(jax.random.fold_in(own, 4), (count // 2,), 0, 1 << 20) % (room + 1)
    lengths = lengths.at[giver].add(-shifted).at[sink].add(shifted)
    items = jnp.searchsorted(jnp.cumsum(lengths), jnp.arange(rows * top), side="right").astype(jnp.int32)
    table = items.reshape(top, rows).T
    table = table[jax.random.permutation(jax.random.fold_in(own, 1), rows)]
    rotation = jax.random.randint(jax.random.fold_in(own, 2), (rows, 1), 0, top)
    return jnp.take_along_axis(table, (jnp.arange(top)[None, :] + rotation) % top, axis=1)


def shares(count, total, reach, skew, full):
    loads = [(1 << 20) // math.isqrt(rank ** skew) + 1 for rank in range(1, count + 1)]
    largest = reach if full else min(reach, max(-(-total // count), total * loads[0] // sum(loads)))
    least = 1 if total - largest >= count - 1 else 0
    given, rest = [largest] + [least] * (count - 1), total - largest - least * (count - 1)
    while rest > 0:
        movable = [i for i in range(1, count) if given[i] < largest] or [i for i in range(1, count) if given[i] < reach]
        mass, budget = sum([loads[i] for i in movable]), rest
        for i in movable:
            extra = min(reach - given[i], max(1, budget * loads[i] // mass), rest)
            given[i] = given[i] + extra
            rest = rest - extra
    return np.array(given)


def noise(rng, dims, deviation, reach, shards=(), held_as=jnp.bfloat16):
    values = deviation * jax.random.normal(rng, dims, jnp.float32)
    if shards:
        values = values * level_of(rng, dims, shards, -0.22, 0.18)
    return jnp.clip(values, -reach, reach).astype(held_as)


def setup_inputs(seed: int = 0) -> dict:
    seeds = jax.random.split(jax.random.key(seed), 7)
    tokens = noise(seeds[0], (TOKENS, D), 1.0, 6.0, ((0, 8),))
    w_gate = noise(seeds[1], (EXPERTS, D, HID), D ** -0.5, 0.09375, ((0, 8), (2, 4)))
    w_up = noise(seeds[2], (EXPERTS, D, HID), D ** -0.5, 0.09375, ((0, 8), (2, 4)))
    w_down = noise(seeds[3], (EXPERTS, HID, D), HID ** -0.5, 0.15625, ((0, 8), (1, 4)))
    route_ids_keys = jax.random.split(jax.random.fold_in(seeds[4], 1), TOKENS // TOK_DEV)
    route_ids_turns = jax.random.permutation(jax.random.fold_in(seeds[4], 3), TOKENS // TOK_DEV)
    route_ids = jax.vmap(lambda own, number: shared_out(jax.random.fold_in(seeds[4], 2), own, number, TOK_DEV, EXPERTS, TOPK, CAP, 2))(route_ids_keys, route_ids_turns).reshape((TOKENS, TOPK))
    route_weight = jnp.clip(jnp.exp(math.log(1.0) - 2.3025851 * jax.random.uniform(seeds[5], (TOKENS, TOPK), jnp.float32) ** level_of(seeds[5], (TOKENS, TOPK), ((0, 8),), -0.2, 0.2)), 0.1, 1.0)
    return dict(tokens=tokens, w_gate=w_gate, w_up=w_up, w_down=w_down, route_ids=route_ids, route_weight=route_weight)


def reference(tokens, w_gate, w_up, w_down, route_ids, route_weight):
    block_count = TOKENS // TOK_DEV
    pair_count = TOK_DEV * TOPK
    block_ids = route_ids.reshape(block_count, pair_count)
    onehot = (block_ids[:, :, None] == jnp.arange(EXPERTS, dtype=jnp.int32)[None, None, :]).astype(jnp.int32)
    slot_index = jnp.sum((jnp.cumsum(onehot, axis=1) - onehot) * onehot, axis=2)
    target_row = (block_ids * CAP + slot_index).astype(jnp.int32)
    owner_token = jnp.repeat(jnp.arange(TOKENS, dtype=jnp.int32), TOPK).reshape(block_count, pair_count)
    block_index = jnp.arange(block_count, dtype=jnp.int32)[:, None]
    token_table = jnp.full((block_count, EXPERTS * CAP), TOKENS, jnp.int32)
    token_table = token_table.at[block_index, target_row].set(owner_token)
    weight_table = jnp.zeros((block_count, EXPERTS * CAP), jnp.float32)
    weight_table = weight_table.at[block_index, target_row].set(route_weight.reshape(block_count, pair_count).astype(jnp.float32))
    token_table = token_table.reshape(block_count, EXPERTS, CAP).transpose(1, 0, 2).reshape(EXPERTS, block_count * CAP)
    weight_table = weight_table.reshape(block_count, EXPERTS, CAP).transpose(1, 0, 2).reshape(EXPERTS, block_count * CAP)
    padded = jnp.concatenate([tokens, jnp.zeros((1, D), tokens.dtype)], axis=0)

    def expert_step(accum, inputs):
        index_rows, weight_rows, gate_w, up_w, down_w = inputs
        picked = padded[index_rows]
        gate_proj = jnp.dot(picked, gate_w, preferred_element_type=jnp.float32)
        up_proj = jnp.dot(picked, up_w, preferred_element_type=jnp.float32)
        hidden = (jax.nn.silu(gate_proj) * up_proj).astype(jnp.bfloat16)
        row_count = hidden.shape[0]
        hidden_groups = hidden.reshape(row_count, N_DP, HPART).astype(jnp.float32)
        down_groups = down_w.reshape(N_DP, HPART, D).astype(jnp.float32)
        partial_value = jnp.einsum("rqh,qhd->qrd", hidden_groups, down_groups).astype(jnp.bfloat16)
        expert_out = jnp.sum(partial_value.astype(jnp.float32), axis=0)
        accum = accum.at[index_rows].add(weight_rows[:, None] * expert_out)
        return accum, None

    start = jnp.zeros((TOKENS + 1, D), jnp.float32)
    total, unused = lax.scan(expert_step, start, (token_table, weight_table, w_gate, w_up, w_down))
    return total[:TOKENS].astype(jnp.bfloat16)
```

```python
import jax
import jax.numpy as jnp
from jax import lax
from jax.experimental import pallas as pl
from jax.experimental.pallas import tpu as pltpu
from jax.sharding import PartitionSpec as P

EXPERTS = 64
TOPK = 8
CAP = 24
MESH = pl.DeviceIdType.MESH


def general(tokens, w_gate, w_up, w_down, route_ids, route_weight):
    tok_rows = tokens.shape[0]
    model_width = tokens.shape[1]
    groups = lax.axis_size("dp")
    peer_count = lax.axis_size("expert")
    local_count = w_gate.shape[0]
    capacity = groups * max(1, 3 * tok_rows * TOPK // (2 * EXPERTS * groups))
    flat_ids = route_ids.reshape(-1)
    onehot = (flat_ids[:, None] == jnp.arange(EXPERTS, dtype=jnp.int32)[None, :]).astype(jnp.int32)
    slot_index = jnp.sum((jnp.cumsum(onehot, axis=0) - onehot) * onehot, axis=1)
    target_row = flat_ids * capacity + slot_index
    owner_token = jnp.repeat(jnp.arange(tok_rows, dtype=jnp.int32), TOPK)
    source_token = (
        jnp.full((EXPERTS * capacity,), tok_rows, jnp.int32).at[target_row].set(owner_token)
    )
    padded = jnp.concatenate([tokens, jnp.zeros((1, model_width), tokens.dtype)], axis=0)
    outgoing = padded[source_token].reshape(EXPERTS, capacity, model_width)
    arrived = lax.all_to_all(outgoing, "expert", split_axis=0, concat_axis=0, tiled=True)
    expert_rows = arrived.reshape(peer_count, local_count, capacity, model_width)
    gate_proj = jnp.einsum(
        "slcd,ldh->slch", expert_rows, w_gate, preferred_element_type=jnp.float32
    )
    up_proj = jnp.einsum("slcd,ldh->slch", expert_rows, w_up, preferred_element_type=jnp.float32)
    hidden = (jax.nn.silu(gate_proj) * up_proj).astype(jnp.bfloat16)
    partial_value = jnp.einsum(
        "slch,lhd->slcd", hidden, w_down, preferred_element_type=jnp.float32
    ).astype(jnp.bfloat16)
    partial_value = partial_value.reshape(peer_count * local_count, capacity, model_width)
    returned = lax.all_to_all(partial_value, "expert", split_axis=0, concat_axis=0, tiled=True)
    picked = returned.reshape(EXPERTS * capacity, model_width)[target_row].reshape(
        tok_rows, TOPK, model_width
    )
    mixed_rows = jnp.sum(route_weight[:, :, None] * picked.astype(jnp.float32), axis=1)
    return lax.psum_scatter(mixed_rows.astype(jnp.bfloat16), "dp", scatter_dimension=1, tiled=True)


def kernel(
    toks, meta, wg, wu, wd, out,
    tok, met, pick, put, rows, rw, hid, gu, dn, down, res, sib, xin, yin, zin,
    tok_r, z_s, sib_s, fx_s, fy_s, rl_s, met_s, met_r, gu_m, dn_m,
    back_s, back_r, x_s, x_r, y_s, y_r, zz_s, zz_r,
):
    n_loc, _, hpart = wg.shape
    tb = toks.shape[0]
    wide = toks.shape[1] // 4
    pair = 2 * CAP
    half = wide // 2
    q = lax.axis_index("dp")
    ex = lax.axis_index("expert")
    z, c = ex // 2, ex % 2
    y, x = q // 2, q % 2
    qx = y * 2 + (1 - x)
    qy = (1 - y) * 2 + x
    qd = 3 - q
    chunk = {0: q, 1: qx, 2: qy, 3: qd}
    other = 1 - c
    twin = z * 2 + other

    def remote(src, dst, s, r, dp, e):
        return pltpu.make_async_remote_copy(
            src_ref=src, dst_ref=dst, send_sem=s, recv_sem=r,
            device_id=(dp, e), device_id_type=MESH,
        )

    def cols(j):
        return pl.ds(pl.multiple_of(j * wide, wide), wide)

    def gu_copy(e, slot):
        return (
            pltpu.make_async_copy(wg.at[e], gu.at[slot, 0], gu_m.at[slot, 0]),
            pltpu.make_async_copy(wu.at[e], gu.at[slot, 1], gu_m.at[slot, 1]),
        )

    order = (3, 1, 2, 0)

    def dn_copy(step):
        col = chunk[order[step // 2]] * wide + (step % 2) * half
        slot = step % 2
        return pltpu.make_async_copy(
            wd.at[:, :, pl.ds(pl.multiple_of(col, half), half)], dn.at[slot], dn_m.at[slot]
        )

    barrier = pltpu.get_barrier_semaphore()
    for k in range(1, 8):
        pl.semaphore_signal(barrier, inc=1, device_id=(q, (ex + k) % 8), device_id_type=MESH)
    for peer in (qx, qy):
        pl.semaphore_signal(barrier, inc=1, device_id=(peer, ex), device_id_type=MESH)
    pl.semaphore_wait(barrier, 9)

    sends = []

    for dz in (1, 2, 3):
        cp = remote(toks.at[:, cols(q)], tok.at[q, ex], z_s.at[dz - 1], tok_r.at[q, ex],
                    q, ((z + dz) % 4) * 2 + c)
        cp.start()
        sends.append(cp)
    for k in range(1, 8):
        cp = remote(meta, met.at[ex], met_s.at[k - 1], met_r.at[ex], q, (ex + k) % 8)
        cp.start()
        sends.append(cp)
    own_meta = pltpu.make_async_copy(meta, met.at[ex], met_r.at[ex])
    own_meta.start()
    own = []
    for j in range(4):
        cp = pltpu.make_async_copy(toks.at[:, pl.ds(j * wide, wide)], tok.at[j, ex],
                                   tok_r.at[j, ex])
        cp.start()
        own.append(cp)
        cp = remote(toks.at[:, pl.ds(j * wide, wide)], tok.at[j, ex], sib_s.at[j, 0],
                    tok_r.at[j, ex], q, twin)
        cp.start()
        sends.append(cp)
    for e in range(2):
        for cp in gu_copy(e, e):
            cp.start()
    for step in range(2):
        dn_copy(step).start()

    def arrive(j, s):
        remote(tok.at[j, s], tok.at[j, s], z_s.at[0], tok_r.at[j, s], q, twin).wait_recv()

    def forward(j, s, sem, dp, e):
        cp = remote(tok.at[j, s], tok.at[j, s], sem, tok_r.at[j, s], dp, e)
        cp.start()
        sends.append(cp)

    for dz in (1, 2, 3):
        s = ((z + 4 - dz) % 4) * 2 + c
        arrive(q, s)
        forward(q, s, fx_s.at[dz - 1], qx, ex)
        forward(q, s, fy_s.at[dz - 1], qy, ex)
        forward(q, s, sib_s.at[0, dz], q, twin)
    rel_in = qx * (1 - c) + qy * c
    rel_out = qy * (1 - c) + qx * c

    own_meta.wait()
    for k in range(1, 8):
        s = (ex + k) % 8
        remote(meta, met.at[s], met_s.at[0], met_r.at[s], q, twin).wait_recv()
    before = (
        lax.broadcasted_iota(jnp.int32, (tb, tb), 0) < lax.broadcasted_iota(jnp.int32, (tb, tb), 1)
    ).astype(jnp.bfloat16)
    spot = lax.broadcasted_iota(jnp.int32, (n_loc, pair, 2 * tb), 1).astype(jnp.float32)

    def build(p, carry):
        vals, wts = [], []
        for k in range(2):
            ids = met[2 * p + k, 0:TOPK]
            wt = met[2 * p + k, TOPK:2 * TOPK]
            ms, ws = [], []
            for e in range(n_loc):
                eq = ids == (ex * n_loc + e).astype(jnp.float32)
                ms.append(jnp.sum(jnp.where(eq, 1.0, 0.0), axis=0, keepdims=True))
                ws.append(jnp.sum(jnp.where(eq, wt, 0.0), axis=0, keepdims=True))
            m = jnp.concatenate(ms, axis=0)
            slot = jnp.dot(m.astype(jnp.bfloat16), before, preferred_element_type=jnp.float32)
            vals.append(jnp.where(m > 0.5, slot + float(CAP * k), -1.0))
            wts.append(jnp.concatenate(ws, axis=0))
        val = jnp.concatenate(vals, axis=1)
        wgt = jnp.concatenate(wts, axis=1)
        hot = jnp.where(val[:, None, :] == spot, 1.0, 0.0)
        rw[:, pl.ds(pl.multiple_of(p * pair, 16), pair), :] = jnp.sum(
            hot * wgt[:, None, :], axis=2, keepdims=True
        )
        hot = hot.reshape(n_loc * pair, 2 * tb)
        pick[p] = hot.astype(jnp.bfloat16)
        put[p] = hot.T.astype(jnp.bfloat16)
        return carry

    lax.fori_loop(0, 4, build, 0)

    for dz in (1, 2, 3):
        s = ((z + 4 - dz) % 4) * 2 + c
        arrive(rel_in, s)
        forward(rel_in, s, rl_s.at[dz - 1], rel_out, ex)
        forward(rel_in, s, sib_s.at[1, dz], q, twin)
        arrive(rel_out, s)
        forward(rel_out, s, sib_s.at[2, dz], q, twin)
    for dz in (1, 2, 3):
        s = ((z + 4 - dz) % 4) * 2 + c
        arrive(qd, s)
        forward(qd, s, sib_s.at[3, dz], q, twin)
    for cp in own:
        cp.wait()

    def fill(i, carry):
        p, j = i // 4, i % 4
        block = tok[j, pl.ds(2 * p, 2)].reshape(2 * tb, wide)
        got = jnp.dot(pick[p], block, preferred_element_type=jnp.float32).astype(jnp.bfloat16)
        rows[:, pl.ds(pl.multiple_of(p * pair, 16), pair), cols(j)] = got.reshape(
            n_loc, pair, wide
        )
        return carry

    for dz in range(4):
        s = ((z + 4 - dz) % 4) * 2 + other
        for j in range(4):
            arrive(j, s)
    lax.fori_loop(0, 16, fill, 0)

    def up(e, carry):
        slot = e % 2
        for cp in gu_copy(e, slot):
            cp.wait()
        a = rows[e]
        g = jnp.dot(a, gu[slot, 0], preferred_element_type=jnp.float32)
        u = jnp.dot(a, gu[slot, 1], preferred_element_type=jnp.float32)
        h = g / (1.0 + jnp.exp(-g)) * u * rw[e]
        hid[e] = h.astype(jnp.bfloat16)

        @pl.when(e + 2 < n_loc)
        def _():
            for cp in gu_copy(e + 2, slot):
                cp.start()

        return carry

    lax.fori_loop(0, n_loc, up, 0)

    def project(step):
        slot = step % 2
        d = order[step // 2]
        dn_copy(step).wait()

        def one(e, carry):
            v = jnp.dot(hid[e], dn[slot, e], preferred_element_type=jnp.float32)
            v = v.astype(jnp.bfloat16).reshape(4, pair, half)
            down[:, pl.ds(pl.multiple_of(e * pair, 16), pair), :] = v
            return carry

        lax.fori_loop(0, n_loc, one, 0)
        if step + 2 < 8:
            dn_copy(step + 2).start()

        def spread(p, carry):
            v = jnp.dot(put[p], down[p], preferred_element_type=jnp.float32).astype(jnp.bfloat16)
            v = v.reshape(2, tb, half)
            res[d, :, p, :, pl.ds((step % 2) * half, half)] = v
            return carry

        lax.fori_loop(0, 4, spread, 0)

    def back(d, p):
        return remote(res.at[d, other, p], sib.at[d, p], back_s.at[d, p], back_r.at[d, p],
                      q, twin)

    def over_x(d, p, slot):
        return remote(res.at[d, c, p], xin.at[slot, p % 2], x_s.at[slot, p % 2],
                      x_r.at[slot, p % 2], qx, ex)

    def over_y(d, p, slot):
        return remote(res.at[d, c, p], yin.at[slot, p % 2], y_s.at[slot, p % 2],
                      y_r.at[slot, p % 2], qy, ex)

    def add(d, p, terms):
        total = res[d, c, p].astype(jnp.float32)
        for t in terms:
            total = total + t[...].astype(jnp.float32)
        return total

    def with_twin(d, p, extra=()):
        back(d, p).wait_recv()
        res[d, c, p] = add(d, p, (sib.at[d, p],) + tuple(extra)).astype(jnp.bfloat16)

    def go(cp):
        cp.start()
        sends.append(cp)

    def stage(d):
        if d == 3:
            for p in (0, 2, 1, 3):
                with_twin(3, p)
                go(over_x(3, p, 0) if p < 2 else over_y(3, p, 0))
        if d == 1:
            for p in (0, 1):
                with_twin(1, p)
                go(over_x(1, p, 1))
        if d == 2:
            for p in (2, 3):
                with_twin(2, p)
                go(over_y(2, p, 1))

    for i, d in enumerate(order):
        project(2 * i)
        project(2 * i + 1)
        for p in range(4):
            go(back(d, p))
        if i >= 1:
            stage(order[i - 1])

    for k in range(2):
        over_x(3, k, 0).wait_recv()
        with_twin(2, k, (xin.at[0, k],))
        go(over_y(2, k, 2))
        over_y(3, 2 + k, 0).wait_recv()
        with_twin(1, 2 + k, (yin.at[0, k],))
        go(over_x(1, 2 + k, 2))

    for p in range(4):
        back(0, p).wait_recv()
    for dz in (2, 1, 3, 0):
        p = (z + dz) % 4
        h, k = p // 2, p % 2
        remote(xin.at[1 + h, k], xin.at[1 + h, k], x_s.at[0, 0], x_r.at[1 + h, k],
               qx, ex).wait_recv()
        remote(yin.at[2 - h, k], yin.at[2 - h, k], y_s.at[0, 0], y_r.at[2 - h, k],
               qy, ex).wait_recv()
        total = add(0, p, (sib.at[0, p], xin.at[1 + h, k], yin.at[2 - h, k]))
        if dz:
            res[0, c, p] = total.astype(jnp.bfloat16)
            go(remote(res.at[0, c, p], zin.at[dz - 1], zz_s.at[dz - 1], zz_r.at[dz - 1],
                      q, p * 2 + c))
    for dz in (1, 2, 3):
        remote(zin.at[dz - 1], zin.at[dz - 1], zz_s.at[0], zz_r.at[dz - 1], q, twin).wait_recv()
        total = total + zin[dz - 1].astype(jnp.float32)
    out[...] = total.astype(jnp.bfloat16)
    for cp in sends:
        cp.wait_send()


def fused(tokens, w_gate, w_up, w_down, route_ids, route_weight):
    tb, width = tokens.shape
    n_loc, _, hpart = w_gate.shape
    wide = width // 4
    half = wide // 2
    bf, f32 = jnp.bfloat16, jnp.float32
    meta = jnp.concatenate([route_ids.astype(f32).T, route_weight.T], axis=0)
    dma = pltpu.SemaphoreType.DMA
    r = 8 * CAP
    hbm = pl.BlockSpec(memory_space=pl.ANY)
    return pl.pallas_call(
        kernel,
        out_shape=jax.ShapeDtypeStruct((tb, wide), bf),
        in_specs=[hbm, pl.BlockSpec(memory_space=pltpu.VMEM), hbm, hbm, hbm],
        out_specs=pl.BlockSpec(memory_space=pltpu.VMEM),
        scratch_shapes=[
            pltpu.VMEM((4, 8, tb, wide), bf),
            pltpu.VMEM((8, 2 * TOPK, tb), f32),
            pltpu.VMEM((4, n_loc * 2 * CAP, 2 * tb), bf),
            pltpu.VMEM((4, 2 * tb, n_loc * 2 * CAP), bf),
            pltpu.VMEM((n_loc, r, width), bf),
            pltpu.VMEM((n_loc, r, 1), f32),
            pltpu.VMEM((n_loc, r, hpart), bf),
            pltpu.VMEM((2, 2, width, hpart), bf),
            pltpu.VMEM((2, n_loc, hpart, half), bf),
            pltpu.VMEM((4, n_loc * 2 * CAP, half), bf),
            pltpu.VMEM((4, 2, 4, tb, wide), bf),
            pltpu.VMEM((4, 4, tb, wide), bf),
            pltpu.VMEM((3, 2, tb, wide), bf),
            pltpu.VMEM((3, 2, tb, wide), bf),
            pltpu.VMEM((3, tb, wide), bf),
            dma((4, 8)), dma((3,)), dma((4, 4)), dma((3,)), dma((3,)), dma((3,)),
            dma((7,)), dma((8,)), dma((2, 2)), dma((2,)),
            dma((4, 4)), dma((4, 4)), dma((3, 2)), dma((3, 2)), dma((3, 2)), dma((3, 2)),
            dma((3,)), dma((3,)),
        ],
        compiler_params=pltpu.CompilerParams(
            collective_id=0, has_side_effects=True, vmem_limit_bytes=63 * 1024 * 1024
        ),
        cost_estimate=pl.CostEstimate(
            flops=20_000_000_000, bytes_accessed=80_000_000, transcendentals=0
        ),
        name="moe",
    )(tokens, meta, w_gate, w_up, w_down)


def solution(mesh):
    small = mesh.shape["dp"] == 4 and mesh.shape["expert"] == 8
    return jax.shard_map(
        fused if small else general,
        mesh=mesh,
        in_specs=(
            P("expert", None),
            P("expert", None, "dp"),
            P("expert", None, "dp"),
            P("expert", "dp", None),
            P("expert", None),
            P("expert", None),
        ),
        out_specs=P("expert", "dp"),
        check_vma=False,
    )
```

```python
import jax
import jax.numpy as jnp
from jax import lax
from jax.experimental import pallas as pl
from jax.experimental.pallas import tpu as pltpu
from jax.sharding import PartitionSpec as P

EXPERTS = 64
TOPK = 8
CAP = 24
MESH = pl.DeviceIdType.MESH


def general(tokens, w_gate, w_up, w_down, route_ids, route_weight):
    tok_rows = tokens.shape[0]
    model_width = tokens.shape[1]
    groups = lax.axis_size("dp")
    peer_count = lax.axis_size("expert")
    local_count = w_gate.shape[0]
    capacity = groups * max(1, 3 * tok_rows * TOPK // (2 * EXPERTS * groups))
    flat_ids = route_ids.reshape(-1)
    onehot = (flat_ids[:, None] == jnp.arange(EXPERTS, dtype=jnp.int32)[None, :]).astype(jnp.int32)
    slot_index = jnp.sum((jnp.cumsum(onehot, axis=0) - onehot) * onehot, axis=1)
    target_row = flat_ids * capacity + slot_index
    owner_token = jnp.repeat(jnp.arange(tok_rows, dtype=jnp.int32), TOPK)
    source_token = (
        jnp.full((EXPERTS * capacity,), tok_rows, jnp.int32).at[target_row].set(owner_token)
    )
    padded = jnp.concatenate([tokens, jnp.zeros((1, model_width), tokens.dtype)], axis=0)
    outgoing = padded[source_token].reshape(EXPERTS, capacity, model_width)
    arrived = lax.all_to_all(outgoing, "expert", split_axis=0, concat_axis=0, tiled=True)
    expert_rows = arrived.reshape(peer_count, local_count, capacity, model_width)
    gate_proj = jnp.einsum(
        "slcd,ldh->slch", expert_rows, w_gate, preferred_element_type=jnp.float32
    )
    up_proj = jnp.einsum("slcd,ldh->slch", expert_rows, w_up, preferred_element_type=jnp.float32)
    hidden = (jax.nn.silu(gate_proj) * up_proj).astype(jnp.bfloat16)
    partial_value = jnp.einsum(
        "slch,lhd->slcd", hidden, w_down, preferred_element_type=jnp.float32
    ).astype(jnp.bfloat16)
    partial_value = partial_value.reshape(peer_count * local_count, capacity, model_width)
    returned = lax.all_to_all(partial_value, "expert", split_axis=0, concat_axis=0, tiled=True)
    picked = returned.reshape(EXPERTS * capacity, model_width)[target_row].reshape(
        tok_rows, TOPK, model_width
    )
    mixed_rows = jnp.sum(route_weight[:, :, None] * picked.astype(jnp.float32), axis=1)
    return lax.psum_scatter(mixed_rows.astype(jnp.bfloat16), "dp", scatter_dimension=1, tiled=True)


def kernel(
    toks, meta, wg, wu, wd, out,
    tok, met, pick, put, rows, rw, hid, gu, dn, down, res, sib, xin, yin, zin,
    tok_r, z_s, sib_s, fx_s, fy_s, rl_s, met_s, met_r, gu_m, dn_m,
    back_s, back_r, x_s, x_r, y_s, y_r, zz_s, zz_r,
):
    n_loc, _, hpart = wg.shape
    tb = toks.shape[0]
    wide = toks.shape[1] // 4
    pair = 2 * CAP
    half = wide // 2
    q = lax.axis_index("dp")
    ex = lax.axis_index("expert")
    z, c = ex // 2, ex % 2
    y, x = q // 2, q % 2
    qx = y * 2 + (1 - x)
    qy = (1 - y) * 2 + x
    qd = 3 - q
    chunk = {0: q, 1: qx, 2: qy, 3: qd}
    other = 1 - c
    twin = z * 2 + other

    def remote(src, dst, s, r, dp, e):
        return pltpu.make_async_remote_copy(
            src_ref=src, dst_ref=dst, send_sem=s, recv_sem=r,
            device_id=(dp, e), device_id_type=MESH,
        )

    def cols(j):
        return pl.ds(pl.multiple_of(j * wide, wide), wide)

    def gu_copy(e, slot):
        return (
            pltpu.make_async_copy(wg.at[e], gu.at[slot, 0], gu_m.at[slot, 0]),
            pltpu.make_async_copy(wu.at[e], gu.at[slot, 1], gu_m.at[slot, 1]),
        )

    order = (3, 1, 2, 0)

    def dn_copy(step):
        col = chunk[order[step // 2]] * wide + (step % 2) * half
        slot = step % 2
        return pltpu.make_async_copy(
            wd.at[:, :, pl.ds(pl.multiple_of(col, half), half)], dn.at[slot], dn_m.at[slot]
        )

    barrier = pltpu.get_barrier_semaphore()
    for k in range(1, 8):
        pl.semaphore_signal(barrier, inc=1, device_id=(q, (ex + k) % 8), device_id_type=MESH)
    for peer in (qx, qy):
        pl.semaphore_signal(barrier, inc=1, device_id=(peer, ex), device_id_type=MESH)
    pl.semaphore_wait(barrier, 9)

    sends = []

    top = z // 2
    source = (top * 2 + 1 - z % 2, 2 - top, 3 - 3 * top)
    inner = z + 1 - 2 * top
    outer = (z + 3 + 2 * top) % 4
    middle = inner + z == 3
    for k in range(1, 8):
        cp = remote(meta, met.at[ex], met_s.at[k - 1], met_r.at[ex], q, (ex + k) % 8)
        cp.start()
        sends.append(cp)
    cp = remote(toks.at[:, cols(q)], tok.at[q, ex], z_s.at[3], tok_r.at[q, ex], q, inner * 2 + c)
    cp.start()
    sends.append(cp)
    outward = remote(toks.at[:, cols(q)], tok.at[q, ex], z_s.at[4], tok_r.at[q, ex],
                     q, outer * 2 + c)

    @pl.when(middle)
    def _():
        outward.start()

    own_meta = pltpu.make_async_copy(meta, met.at[ex], met_r.at[ex])
    own_meta.start()
    own = []
    for j in range(4):
        cp = pltpu.make_async_copy(toks.at[:, pl.ds(j * wide, wide)], tok.at[j, ex],
                                   tok_r.at[j, ex])
        cp.start()
        own.append(cp)
        cp = remote(toks.at[:, pl.ds(j * wide, wide)], tok.at[j, ex], sib_s.at[j, 0],
                    tok_r.at[j, ex], q, twin)
        cp.start()
        sends.append(cp)
    for e in range(2):
        for cp in gu_copy(e, e):
            cp.start()
    for step in range(2):
        dn_copy(step).start()

    def arrive(j, s):
        remote(tok.at[j, s], tok.at[j, s], z_s.at[0], tok_r.at[j, s], q, twin).wait_recv()

    def forward(j, s, sem, dp, e):
        cp = remote(tok.at[j, s], tok.at[j, s], sem, tok_r.at[j, s], dp, e)
        cp.start()
        sends.append(cp)

    passed = []

    def from_line(n):
        s = source[n] * 2 + c
        arrive(q, s)
        cp = remote(tok.at[q, s], tok.at[q, s], z_s.at[n], tok_r.at[q, s],
                    q, (outer if n else inner) * 2 + c)

        @pl.when(middle)
        def _():
            cp.start()

        passed.append(cp)
        forward(q, s, fx_s.at[n], qx, ex)
        forward(q, s, fy_s.at[n], qy, ex)
        forward(q, s, sib_s.at[0, n + 1], q, twin)

    rel_in = qx * (1 - c) + qy * c
    rel_out = qy * (1 - c) + qx * c

    own_meta.wait()
    for k in range(1, 8):
        s = (ex + k) % 8
        remote(meta, met.at[s], met_s.at[0], met_r.at[s], q, twin).wait_recv()
    before = (
        lax.broadcasted_iota(jnp.int32, (tb, tb), 0) < lax.broadcasted_iota(jnp.int32, (tb, tb), 1)
    ).astype(jnp.bfloat16)
    spot = lax.broadcasted_iota(jnp.int32, (n_loc, pair, 2 * tb), 1).astype(jnp.float32)

    def build(p, carry):
        vals, wts = [], []
        for k in range(2):
            ids = met[2 * p + k, 0:TOPK]
            wt = met[2 * p + k, TOPK:2 * TOPK]
            ms, ws = [], []
            for e in range(n_loc):
                eq = ids == (ex * n_loc + e).astype(jnp.float32)
                ms.append(jnp.sum(jnp.where(eq, 1.0, 0.0), axis=0, keepdims=True))
                ws.append(jnp.sum(jnp.where(eq, wt, 0.0), axis=0, keepdims=True))
            m = jnp.concatenate(ms, axis=0)
            slot = jnp.dot(m.astype(jnp.bfloat16), before, preferred_element_type=jnp.float32)
            vals.append(jnp.where(m > 0.5, slot + float(CAP * k), -1.0))
            wts.append(jnp.concatenate(ws, axis=0))
        val = jnp.concatenate(vals, axis=1)
        wgt = jnp.concatenate(wts, axis=1)
        hot = jnp.where(val[:, None, :] == spot, 1.0, 0.0)
        rw[:, pl.ds(pl.multiple_of(p * pair, 16), pair), :] = jnp.sum(
            hot * wgt[:, None, :], axis=2, keepdims=True
        )
        hot = hot.reshape(n_loc * pair, 2 * tb)
        pick[p] = hot.astype(jnp.bfloat16)
        put[p] = hot.T.astype(jnp.bfloat16)
        return carry

    from_line(0)
    lax.fori_loop(0, 4, build, 0)

    def from_plane(n):
        s = source[n] * 2 + c
        arrive(rel_in, s)
        forward(rel_in, s, rl_s.at[n], rel_out, ex)
        forward(rel_in, s, sib_s.at[1, n + 1], q, twin)
        arrive(rel_out, s)
        forward(rel_out, s, sib_s.at[2, n + 1], q, twin)

    def from_corner(n):
        s = source[n] * 2 + c
        arrive(qd, s)
        forward(qd, s, sib_s.at[3, n + 1], q, twin)

    def fill(p):
        for j in range(4):
            arrive(j, p * 2 + other)

        def one(j, carry):
            block = tok[j, pl.ds(2 * p, 2)].reshape(2 * tb, wide)
            got = jnp.dot(pick[p], block, preferred_element_type=jnp.float32)
            rows[:, pl.ds(pl.multiple_of(p * pair, 16), pair), cols(j)] = got.astype(
                jnp.bfloat16
            ).reshape(n_loc, pair, wide)
            return carry

        lax.fori_loop(0, 4, one, 0)

    from_line(1)
    from_plane(0)
    for cp in own:
        cp.wait()
    fill(z)
    from_line(2)
    from_plane(1)
    from_corner(0)
    from_plane(2)
    fill(source[0])
    from_corner(1)
    from_corner(2)
    fill(source[1])
    fill(source[2])

    def up(e, carry):
        slot = e % 2
        for cp in gu_copy(e, slot):
            cp.wait()
        a = rows[e]
        g = jnp.dot(a, gu[slot, 0], preferred_element_type=jnp.float32)
        u = jnp.dot(a, gu[slot, 1], preferred_element_type=jnp.float32)
        h = g / (1.0 + jnp.exp(-g)) * u * rw[e]
        hid[e] = h.astype(jnp.bfloat16)

        @pl.when(e + 2 < n_loc)
        def _():
            for cp in gu_copy(e + 2, slot):
                cp.start()

        return carry

    lax.fori_loop(0, n_loc, up, 0)

    def project(step):
        slot = step % 2
        d = order[step // 2]
        dn_copy(step).wait()

        def one(e, carry):
            v = jnp.dot(hid[e], dn[slot, e], preferred_element_type=jnp.float32)
            v = v.astype(jnp.bfloat16).reshape(4, pair, half)
            down[:, pl.ds(pl.multiple_of(e * pair, 16), pair), :] = v
            return carry

        lax.fori_loop(0, n_loc, one, 0)
        if step + 2 < 8:
            dn_copy(step + 2).start()

        def spread(p, carry):
            v = jnp.dot(put[p], down[p], preferred_element_type=jnp.float32).astype(jnp.bfloat16)
            v = v.reshape(2, tb, half)
            res[d, :, p, :, pl.ds((step % 2) * half, half)] = v
            return carry

        lax.fori_loop(0, 4, spread, 0)

    def back(d, p):
        return remote(res.at[d, other, p], sib.at[d, p], back_s.at[d, p], back_r.at[d, p],
                      q, twin)

    def over_x(d, p, slot):
        return remote(res.at[d, c, p], xin.at[slot, p % 2], x_s.at[slot, p % 2],
                      x_r.at[slot, p % 2], qx, ex)

    def over_y(d, p, slot):
        return remote(res.at[d, c, p], yin.at[slot, p % 2], y_s.at[slot, p % 2],
                      y_r.at[slot, p % 2], qy, ex)

    def add(d, p, terms):
        total = res[d, c, p].astype(jnp.float32)
        for t in terms:
            total = total + t[...].astype(jnp.float32)
        return total

    def with_twin(d, p, extra=()):
        back(d, p).wait_recv()
        res[d, c, p] = add(d, p, (sib.at[d, p],) + tuple(extra)).astype(jnp.bfloat16)

    def go(cp):
        cp.start()
        sends.append(cp)

    def first_leg(d, p):
        with_twin(d, p)
        slot = 0 if d == 3 else 1
        go(over_x(d, p, slot) if p < 2 else over_y(d, p, slot))

    def second_leg(p):
        k = p % 2
        if p < 2:
            over_x(3, p, 0).wait_recv()
            with_twin(2, p, (xin.at[0, k],))
            go(over_y(2, p, 2))
        else:
            over_y(3, p, 0).wait_recv()
            with_twin(1, p, (yin.at[0, k],))
            go(over_x(1, p, 2))

    def finish(p):
        k = p % 2
        last_x, last_y = (1, 2) if p < 2 else (2, 1)
        over_x(0, p, last_x).wait_recv()
        over_y(0, p, last_y).wait_recv()
        with_twin(0, p, (xin.at[last_x, k], yin.at[last_y, k]))
        slot = (z + 3 - p) % 4
        cp = remote(res.at[0, c, p], zin.at[slot % 3], zz_s.at[p], zz_r.at[slot % 3], q, p * 2 + c)

        @pl.when(z != p)
        def _():
            cp.start()

        ends.append((p, cp))

    ends = []
    early, late = (0, 3), (1, 2)
    for i, d in enumerate(order):
        project(2 * i)
        project(2 * i + 1)
        for p in (0, 3, 1, 2):
            go(back(d, p))
        if i == 1:
            for p in early:
                first_leg(3, p)
        if i == 2:
            first_leg(1, early[0])
    first_leg(2, early[1])
    for p in early:
        second_leg(p)
    for p in late:
        first_leg(3, p)
    first_leg(1, late[0])
    first_leg(2, late[1])
    for p in early:
        finish(p)
    for p in late:
        second_leg(p)
    for p in late:
        finish(p)
    total = res[0, c, z].astype(jnp.float32)
    for dz in (1, 2, 3):
        remote(zin.at[dz - 1], zin.at[dz - 1], zz_s.at[0], zz_r.at[dz - 1], q, twin).wait_recv()
        total = total + zin[dz - 1].astype(jnp.float32)
    out[...] = total.astype(jnp.bfloat16)
    for cp in sends:
        cp.wait_send()
    for p, cp in ends:

        @pl.when(z != p)
        def _():
            cp.wait_send()

    @pl.when(middle)
    def _():
        outward.wait_send()
        for cp in passed:
            cp.wait_send()


def fused(tokens, w_gate, w_up, w_down, route_ids, route_weight):
    tb, width = tokens.shape
    n_loc, _, hpart = w_gate.shape
    wide = width // 4
    half = wide // 2
    bf, f32 = jnp.bfloat16, jnp.float32
    meta = jnp.concatenate([route_ids.astype(f32).T, route_weight.T], axis=0)
    dma = pltpu.SemaphoreType.DMA
    r = 8 * CAP
    hbm = pl.BlockSpec(memory_space=pl.ANY)
    return pl.pallas_call(
        kernel,
        out_shape=jax.ShapeDtypeStruct((tb, wide), bf),
        in_specs=[hbm, pl.BlockSpec(memory_space=pltpu.VMEM), hbm, hbm, hbm],
        out_specs=pl.BlockSpec(memory_space=pltpu.VMEM),
        scratch_shapes=[
            pltpu.VMEM((4, 8, tb, wide), bf),
            pltpu.VMEM((8, 2 * TOPK, tb), f32),
            pltpu.VMEM((4, n_loc * 2 * CAP, 2 * tb), bf),
            pltpu.VMEM((4, 2 * tb, n_loc * 2 * CAP), bf),
            pltpu.VMEM((n_loc, r, width), bf),
            pltpu.VMEM((n_loc, r, 1), f32),
            pltpu.VMEM((n_loc, r, hpart), bf),
            pltpu.VMEM((2, 2, width, hpart), bf),
            pltpu.VMEM((2, n_loc, hpart, half), bf),
            pltpu.VMEM((4, n_loc * 2 * CAP, half), bf),
            pltpu.VMEM((4, 2, 4, tb, wide), bf),
            pltpu.VMEM((4, 4, tb, wide), bf),
            pltpu.VMEM((3, 2, tb, wide), bf),
            pltpu.VMEM((3, 2, tb, wide), bf),
            pltpu.VMEM((3, tb, wide), bf),
            dma((4, 8)), dma((5,)), dma((4, 4)), dma((3,)), dma((3,)), dma((3,)),
            dma((7,)), dma((8,)), dma((2, 2)), dma((2,)),
            dma((4, 4)), dma((4, 4)), dma((3, 2)), dma((3, 2)), dma((3, 2)), dma((3, 2)),
            dma((4,)), dma((3,)),
        ],
        compiler_params=pltpu.CompilerParams(
            collective_id=0, has_side_effects=True, vmem_limit_bytes=63 * 1024 * 1024
        ),
        cost_estimate=pl.CostEstimate(
            flops=20_000_000_000, bytes_accessed=80_000_000, transcendentals=0
        ),
        name="moe",
    )(tokens, meta, w_gate, w_up, w_down)


def solution(mesh):
    small = mesh.shape["dp"] == 4 and mesh.shape["expert"] == 8
    return jax.shard_map(
        fused if small else general,
        mesh=mesh,
        in_specs=(
            P("expert", None),
            P("expert", None, "dp"),
            P("expert", None, "dp"),
            P("expert", "dp", None),
            P("expert", None),
            P("expert", None),
        ),
        out_specs=P("expert", "dp"),
        check_vma=False,
    )
```
